32 devices in a mesh: groups: 2 (over y), aa: 4 (over z), ba: 2 (over x), col: 2 (over core).
Axes of the slice: x: 2, y: 2, z: 4, core: 2. Of those that a mesh axis runs over, the one named last changes fastest.
Arguments:
- tokens: bfloat16 [512, 8192], P(('groups', 'col', 'ba'), 'aa'), parts along dimension 0, may hold values from -640 to 640
- norm_gain: bfloat16 [8192], P('aa'), may hold values from 0.099609375 to 1.8984375
- gate_weight: bfloat16 [8192, 14336], P('aa', ('ba', 'col')), may hold values from -0.0625 to 0.0625
- up_weight: bfloat16 [8192, 14336], P('aa', ('ba', 'col')), may hold values from -0.0625 to 0.0625
Outputs:
- hidden: bfloat16 [512, 14336], P(('groups', 'col', 'aa'), 'ba'), parts along dimension 0
The draws below stay inside these ranges and needn't reach their ends.
There are 2 independent parts, one for each index of `groups`. The reference program is written for one: setup_inputs(seed, part) draws one part's arguments, and reference() takes and returns one part's arrays. A program takes and returns all parts, laid end to end along the dimension named above; an argument that names none is the same for every part. Nothing has to cross between parts.
All inputs are finite; a program needn't handle non-finite values.
Results may differ from the reference program's by a relative error of at most 0.015.
Values may be sent and summed in bfloat16 or wider, within the bound.
A program may use at most 192 MiB of HBM per device.

```python
import math
import jax
import jax.numpy as jnp
from jax import lax

D = 8192
FF = 14336
TOKENS = 256
N_AA = 4


def draw_tokens(key, part):
    key = jax.random.fold_in(key, 11)
    key_base, key_cols, key_rows = jax.random.split(key, 3)
    position = jnp.arange(D, dtype=jnp.float32) / D
    col_scale = (1.0 + 2.0 * position) * jnp.exp(jax.random.uniform(key_cols, (D,), jnp.float32, 0.0, math.log(4.0)))
    row_scale = jnp.exp(jax.random.uniform(key_rows, (TOKENS, 1), jnp.float32, 0.0, math.log(10.0)))
    base = jnp.clip(jax.random.normal(key_base, (TOKENS, D), jnp.float32), -5.0, 5.0)
    return (base * row_scale * col_scale).astype(jnp.bfloat16)


def block_scale(own_key, dims, cuts, low, largest):
    def one(axis_at, blocks):
        heights = jax.random.uniform(jax.random.fold_in(jax.random.fold_in(own_key, 6), axis_at), (blocks,), jnp.float32, low / len(cuts), largest / len(cuts))
        return jnp.repeat(jnp.exp(heights), dims[axis_at] // blocks).reshape((-1,) + (1,) * (len(dims) - axis_at - 1))

    loudness = one(*cuts[0])
    for cut in cuts[1:]:
        loudness = loudness * one(*cut)
    return loudness


def noise(stream_key, dims, deviation, bound, cuts=(), held_as=jnp.bfloat16):
    result = jax.random.normal(stream_key, dims, jnp.float32) * deviation
    if len(cuts) > 0:
        result = block_scale(stream_key, dims, cuts, -0.22, 0.18) * result
    return jnp.clip(result, min=-bound, max=bound).astype(held_as)


def setup_inputs(seed: int = 0, part: int = 0) -> dict:
    splits = jax.random.split(jax.random.key(seed), 5)
    part_splits = jax.random.split(jax.random.fold_in(splits[4], part), 5)
    tokens = draw_tokens(jax.random.fold_in(jax.random.fold_in(splits[4], part), 71), part)
    norm_gain = jnp.clip(1.0 + 0.18 * jax.random.normal(splits[1], (D,), jnp.float32), 0.099609375, 1.8984375).astype(jnp.bfloat16)
    gate_weight = noise(splits[2], (D, FF), D ** -0.5, 0.0625, ((0, 4), (1, 4)))
    up_weight = noise(splits[3], (D, FF), D ** -0.5, 0.0625, ((0, 4), (1, 4)))
    return dict(tokens=tokens, norm_gain=norm_gain, gate_weight=gate_weight, up_weight=up_weight)


epsilon = 1e-05

def reference(tokens, norm_gain, gate_weight, up_weight):
    values = tokens.astype(jnp.float32)
    squares = lax.optimization_barrier(jnp.sum(values * values, axis=1, keepdims=True))
    normed = (values * lax.rsqrt(squares / D + epsilon) * norm_gain.astype(jnp.float32)).astype(jnp.bfloat16)
    width_block = D // N_AA
    gate_sum = jnp.zeros((TOKENS, FF), jnp.float32)
    up_sum = jnp.zeros((TOKENS, FF), jnp.float32)
    for index_block in range(N_AA):
        lower = index_block * width_block
        left_block = normed[:, lower:lower + width_block]
        gate_part = jnp.dot(left_block, gate_weight[lower:lower + width_block], preferred_element_type=jnp.float32).astype(jnp.bfloat16)
        up_part = jnp.dot(left_block, up_weight[lower:lower + width_block], preferred_element_type=jnp.float32).astype(jnp.bfloat16)
        gate_sum = gate_sum + lax.optimization_barrier(gate_part).astype(jnp.float32)
        up_sum = up_sum + lax.optimization_barrier(up_part).astype(jnp.float32)
    return (jax.nn.silu(gate_sum) * up_sum).astype(jnp.bfloat16)
```

```python
import functools

import jax
import jax.numpy as jnp
from jax import lax
from jax.experimental import pallas as pl
from jax.experimental.pallas import tpu as pltpu
from jax.sharding import PartitionSpec as P

MESH = pl.DeviceIdType.MESH
EPSILON = 1e-05
LAG = 2


def kernel(sizes, tokens, gain, gate_w, up_w, out, raw, scaled, gate_v, up_v, acc, recv, send,
           hid, sq_own, sq_recv, factor, w_sem, own_sem, x_send, x_recv, c_send, c_recv,
           part_send, part_recv, sq_send, sq_rsem, hid_send, out_recv):
    n, n_ba, n_col, tiles = sizes
    a, b, c = lax.axis_index("aa"), lax.axis_index("ba"), lax.axis_index("col")
    own_rows, depth = tokens.shape
    width = gate_w.shape[1]
    tu = width // tiles
    half = scaled.shape[0] // 2
    out_rows = out.shape[0]
    dests = n // 2

    def start_of(bb, cc):
        per_half = n_ba // 2
        row = (bb // per_half) * half + cc * (half // n_col) + (bb % per_half) * own_rows
        return pl.multiple_of(row, own_rows)

    def block(bb, cc):
        return raw.at[pl.ds(start_of(bb, cc), own_rows)]

    def weight_copies(j):
        cols = pl.ds(pl.multiple_of(j * tu, tu), tu)
        return (pltpu.make_async_copy(gate_w.at[:, cols], gate_v.at[j], w_sem.at[0, j]),
                pltpu.make_async_copy(up_w.at[:, cols], up_v.at[j], w_sem.at[1, j]))

    barrier = pltpu.get_barrier_semaphore()
    peers = 0
    for da in range(n):
        for dc in range(n_col):
            if da or dc:
                pl.semaphore_signal(
                    barrier, inc=1, device_id_type=MESH,
                    device_id={"aa": lax.rem(a + da, n), "col": lax.rem(c + dc, n_col)})
                peers += 1
    for db in range(1, n_ba):
        pl.semaphore_signal(barrier, inc=1, device_id={"ba": lax.rem(b + db, n_ba)},
                            device_id_type=MESH)
        peers += 1

    own = pltpu.make_async_copy(tokens, block(b, c), own_sem)
    own.start()

    @pl.loop(0, tiles)
    def _(j):
        for copy in weight_copies(j):
            copy.start()

    pl.semaphore_wait(barrier, peers)

    def to_chip(db):
        return pltpu.make_async_remote_copy(
            tokens, block(b, c), x_send.at[db], x_recv.at[db],
            device_id={"ba": lax.rem(b + db, n_ba)}, device_id_type=MESH)

    def from_chip(db):
        return pltpu.make_async_remote_copy(
            tokens, block(lax.rem(b - db + n_ba, n_ba), c), x_send.at[db], x_recv.at[db],
            device_id={"ba": lax.rem(b + db, n_ba)}, device_id_type=MESH)

    def to_core(db, dc):
        spot = block(lax.rem(b - db + n_ba, n_ba), c)
        return pltpu.make_async_remote_copy(
            tokens if db == 0 else spot, spot, c_send.at[db, dc], c_recv.at[db, dc],
            device_id={"col": lax.rem(c + dc, n_col)}, device_id_type=MESH)

    def from_core(db, dc):
        spot = block(lax.rem(b - db + n_ba, n_ba), lax.rem(c - dc + n_col, n_col))
        return pltpu.make_async_remote_copy(
            tokens, spot, c_send.at[db, dc], c_recv.at[db, dc],
            device_id={"col": lax.rem(c + dc, n_col)}, device_id_type=MESH)

    for db in range(1, n_ba):
        to_chip(db).start()
    for dc in range(1, n_col):
        to_core(0, dc).start()
    for db in range(1, n_ba):
        from_chip(db).wait_recv()
        for dc in range(1, n_col):
            to_core(db, dc).start()
    own.wait()
    for db in range(n_ba):
        for dc in range(1, n_col):
            from_core(db, dc).wait_recv()

    @pl.loop(0, 2 * half // 128)
    def _(r):
        rows = pl.ds(pl.multiple_of(r * 128, 128), 128)
        total = jnp.zeros((128, 128), jnp.float32)
        for q in range(depth // 128):
            cols = slice(q * 128, (q + 1) * 128)
            value = raw[rows, cols].astype(jnp.float32)
            total = total + value * value
            scaled[rows, cols] = (value * gain[:, cols].astype(jnp.float32)).astype(jnp.bfloat16)
        line = jnp.sum(jnp.transpose(total), axis=0, keepdims=True)
        per = half // 128
        sq_own[r // per, r % per] = jnp.broadcast_to(line, (8, 128))

    def sq_copy(h, slot):
        return pltpu.make_async_remote_copy(
            sq_own.at[h], sq_recv.at[slot], sq_send.at[h], sq_rsem.at[slot],
            device_id={"aa": h * (n - 1)}, device_id_type=MESH)

    for h in range(2):
        @pl.when(a != h * (n - 1))
        def _():
            sq_copy(h, a).start()

    def part_copy(h, k):
        to = jnp.maximum(a - 1, 0) if h == 0 else jnp.minimum(a + 1, n - 1)
        return pltpu.make_async_remote_copy(
            send.at[h, k], recv.at[h, k], part_send.at[h, k], part_recv.at[h, k],
            device_id={"aa": to}, device_id_type=MESH)

    def hid_copy(h, k, dd, cc):
        index = cc * dests + dd
        spot = out.at[:, pl.ds(pl.multiple_of(c * width + k * tu, tu), tu)]
        return pltpu.make_async_remote_copy(
            hid.at[k, pl.ds(index * out_rows, out_rows)], spot,
            hid_send.at[k, index], out_recv.at[k, c],
            device_id={"aa": h * dests + dd, "col": cc}, device_id_type=MESH)

    def mine(h, dd, cc):
        return (c == cc) if dd == h * (dests - 1) else False

    def hop(h):
        return n - 1 - a if h == 0 else a

    def handle(h, k):
        here = hop(h)
        rows = slice(h * half, (h + 1) * half)

        @pl.when(here > 0)
        def _():
            part_copy(h, k).wait_recv()

        @pl.when(here == 0)
        def _():
            send[h, k] = acc[k, rows, :].astype(jnp.bfloat16)

        @pl.when((here > 0) & (here < n - 1))
        def _():
            send[h, k] = (acc[k, rows, :] + recv[h, k].astype(jnp.float32)).astype(jnp.bfloat16)

        @pl.when(here < n - 1)
        def _():
            part_copy(h, k).start()

        @pl.when(here == n - 1)
        def _():
            @pl.when(k == 0)
            def _():
                total = sq_own[h]
                for d in range(n):
                    if d != h * (n - 1):
                        sq_copy(h, d).wait_recv()
                        total = total + sq_recv[d]
                rate = lax.rsqrt(total / (depth * n) + EPSILON)
                for r in range(half // 128):
                    factor[r * 128:(r + 1) * 128, :] = jnp.transpose(
                        jnp.broadcast_to(rate[r, 0:1, :], (128, 128)))

            scale = factor[...]
            for q in range(tu // 128):
                at = slice(q * 128, (q + 1) * 128)
                late = slice(tu + q * 128, tu + (q + 1) * 128)
                gate = (acc[k, rows, at] + recv[h, k, :, at].astype(jnp.float32)) * scale
                up = (acc[k, rows, late] + recv[h, k, :, late].astype(jnp.float32)) * scale
                hid[k, :, at] = (gate / (1.0 + jnp.exp(-gate)) * up).astype(jnp.bfloat16)
            for cc in range(n_col):
                for dd in range(dests):
                    own_block = mine(h, dd, cc)
                    if own_block is False:
                        hid_copy(h, k, dd, cc).start()
                    else:
                        @pl.when(own_block)
                        def _():
                            index = cc * dests + dd
                            out[:, pl.ds(pl.multiple_of(c * width + k * tu, tu), tu)] = hid[
                                k, index * out_rows:(index + 1) * out_rows, :]

                        @pl.when(jnp.logical_not(own_block))
                        def _():
                            hid_copy(h, k, dd, cc).start()

    @pl.loop(0, tiles + (n - 1) * LAG)
    def _(s):
        @pl.when(s < tiles)
        def _():
            for copy in weight_copies(s):
                copy.wait()
            acc[s, :, :tu] = jnp.dot(scaled[...], gate_v[s], preferred_element_type=jnp.float32)
            acc[s, :, tu:] = jnp.dot(scaled[...], up_v[s], preferred_element_type=jnp.float32)

        for h in range(2):
            k = s - hop(h) * LAG

            @pl.when((k >= 0) & (k < tiles))
            def _():
                handle(h, k)

    for db in range(1, n_ba):
        to_chip(db).wait_send()
    for db in range(n_ba):
        for dc in range(1, n_col):
            to_core(db, dc).wait_send()
    for h in range(2):
        @pl.when(a != h * (n - 1))
        def _():
            sq_copy(h, a).wait_send()

    finisher = (a == 0) | (a == n - 1)

    @pl.loop(0, tiles)
    def _(k):
        for h in range(2):
            @pl.when(hop(h) < n - 1)
            def _():
                part_copy(h, k).wait_send()

            @pl.when(hop(h) == n - 1)
            def _():
                for cc in range(n_col):
                    for dd in range(dests):
                        @pl.when(jnp.logical_not(mine(h, dd, cc)))
                        def _():
                            hid_copy(h, k, dd, cc).wait_send()

        for cc in range(n_col):
            @pl.when(jnp.logical_not(finisher & (c == cc)))
            def _():
                spot = out.at[:, pl.ds(pl.multiple_of(cc * width + k * tu, tu), tu)]
                pltpu.make_async_remote_copy(
                    hid.at[k, pl.ds(0, out_rows)], spot, hid_send.at[k, 0], out_recv.at[k, cc],
                    device_id={"col": cc}, device_id_type=MESH).wait_recv()


def shards(sizes, tokens, norm_gain, gate_weight, up_weight):
    n, n_ba, n_col, tiles = sizes
    own_rows, depth = tokens.shape
    width = gate_weight.shape[1]
    tu = width // tiles
    rows = own_rows * n_ba * n_col
    half = rows // 2
    out_rows = rows // (n * n_col)
    bf16, f32 = jnp.bfloat16, jnp.float32
    dma = pltpu.SemaphoreType.DMA
    any_space = pl.BlockSpec(memory_space=pl.ANY)
    vmem = pl.BlockSpec(memory_space=pltpu.VMEM)
    flops = 2 * rows * depth * 2 * width
    return pl.pallas_call(
        functools.partial(kernel, sizes),
        out_shape=jax.ShapeDtypeStruct((out_rows, width * n_col), bf16),
        in_specs=[any_space, vmem, any_space, any_space],
        out_specs=vmem,
        scratch_shapes=[
            pltpu.VMEM((rows, depth), bf16),
            pltpu.VMEM((rows, depth), bf16),
            pltpu.VMEM((tiles, depth, tu), bf16),
            pltpu.VMEM((tiles, depth, tu), bf16),
            pltpu.VMEM((tiles, rows, 2 * tu), f32),
            pltpu.VMEM((2, tiles, half, 2 * tu), bf16),
            pltpu.VMEM((2, tiles, half, 2 * tu), bf16),
            pltpu.VMEM((tiles, half, tu), bf16),
            pltpu.VMEM((2, half // 128, 8, 128), f32),
            pltpu.VMEM((n, half // 128, 8, 128), f32),
            pltpu.VMEM((half, 128), f32),
            dma((2, tiles)),
            dma,
            dma((n_ba,)),
            dma((n_ba,)),
            dma((n_ba, n_col)),
            dma((n_ba, n_col)),
            dma((2, tiles)),
            dma((2, tiles)),
            dma((2,)),
            dma((n,)),
            dma((tiles, n // 2 * n_col)),
            dma((tiles, n_col)),
        ],
        compiler_params=pltpu.CompilerParams(
            collective_id=0, has_side_effects=True, vmem_limit_bytes=60 * 1024 * 1024),
        cost_estimate=pl.CostEstimate(
            flops=flops, bytes_accessed=4 * depth * width, transcendentals=half * width),
    )(tokens, norm_gain.reshape(1, depth), gate_weight, up_weight)


def solution(mesh):
    def run(tokens, norm_gain, gate_weight, up_weight):
        n, n_ba, n_col = mesh.shape["aa"], mesh.shape["ba"], mesh.shape["col"]
        width = gate_weight.shape[1] // (n_ba * n_col)
        tu = 256 if width % 256 == 0 and width > 1024 else 128
        sizes = (n, n_ba, n_col, width // tu)
        return jax.shard_map(
            functools.partial(shards, sizes),
            mesh=mesh,
            in_specs=(
                P(("groups", "col", "ba"), "aa"),
                P("aa"),
                P("aa", ("ba", "col")),
                P("aa", ("ba", "col")),
            ),
            out_specs=P(("groups", "col", "aa"), "ba"),
            check_vma=False,
        )(tokens, norm_gain, gate_weight, up_weight)

    return run
```

```python
import functools

import jax
import jax.numpy as jnp
from jax import lax
from jax.experimental import pallas as pl
from jax.experimental.pallas import tpu as pltpu
from jax.sharding import PartitionSpec as P

MESH = pl.DeviceIdType.MESH
EPSILON = 1e-05
LAG = 2
AHEAD = 6


def kernel(sizes, tokens, gain, gate_w, up_w, out, raw, scaled, gate_v, up_v, acc, recv, send,
           hid, sq_own, sq_recv, factor, w_sem, own_sem, x_send, x_recv, c_send, c_recv,
           part_send, part_recv, sq_send, sq_rsem, hid_send, out_recv):
    n, n_ba, n_col, tiles = sizes
    a, b, c = lax.axis_index("aa"), lax.axis_index("ba"), lax.axis_index("col")
    own_rows, depth = tokens.shape
    width = gate_w.shape[1]
    tu = width // tiles
    half = scaled.shape[0] // 2
    out_rows = out.shape[0]
    dests = n // 2
    ahead = min(AHEAD, tiles)
    late = tiles - 3 if n > 2 else tiles

    def start_of(bb, cc):
        per_half = n_ba // 2
        row = (bb // per_half) * half + cc * (half // n_col) + (bb % per_half) * own_rows
        return pl.multiple_of(row, own_rows)

    def block(bb, cc):
        return raw.at[pl.ds(start_of(bb, cc), own_rows)]

    def weight_copies(j):
        cols = pl.ds(pl.multiple_of(j * tu, tu), tu)
        return (pltpu.make_async_copy(gate_w.at[:, cols], gate_v.at[j], w_sem.at[0, j]),
                pltpu.make_async_copy(up_w.at[:, cols], up_v.at[j], w_sem.at[1, j]))

    barrier = pltpu.get_barrier_semaphore()
    peers = 0
    for da in range(n):
        for dc in range(n_col):
            if da or dc:
                pl.semaphore_signal(
                    barrier, inc=1, device_id_type=MESH,
                    device_id={"aa": lax.rem(a + da, n), "col": lax.rem(c + dc, n_col)})
                peers += 1
    for db in range(1, n_ba):
        pl.semaphore_signal(barrier, inc=1, device_id={"ba": lax.rem(b + db, n_ba)},
                            device_id_type=MESH)
        peers += 1

    own = pltpu.make_async_copy(tokens, block(b, c), own_sem)
    own.start()

    @pl.loop(0, tiles)
    def _(j):
        for copy in weight_copies(j):
            copy.start()

    pl.semaphore_wait(barrier, peers)

    def piece(ref, p):
        return ref.at[pl.ds(p * (own_rows // 2), own_rows // 2)]

    def back(i, d, count):
        return lax.rem(i - d + count, count)

    def to_chip(db, p, source=None):
        spot = block(b if source is None else source, c)
        return pltpu.make_async_remote_copy(
            piece(tokens, p), piece(spot, p), x_send.at[db, p], x_recv.at[db, p],
            device_id={"ba": lax.rem(b + db, n_ba)}, device_id_type=MESH)

    def to_core(db, dc, p):
        spot = piece(block(back(b, db, n_ba), c), p)
        return pltpu.make_async_remote_copy(
            piece(tokens, p) if db == 0 else spot, spot, c_send.at[db, dc, p],
            c_recv.at[db, dc, p],
            device_id={"col": lax.rem(c + dc, n_col)}, device_id_type=MESH)

    def from_core(db, dc, p):
        spot = piece(block(back(b, db, n_ba), back(c, dc, n_col)), p)
        return pltpu.make_async_remote_copy(
            piece(tokens, p), spot, c_send.at[db, dc, p], c_recv.at[db, dc, p],
            device_id={"col": lax.rem(c + dc, n_col)}, device_id_type=MESH)

    def forward(p):
        for db in range(1, n_ba):
            to_chip(db, p, back(b, db, n_ba)).wait_recv()
            for dc in range(1, n_col):
                to_core(db, dc, p).start()

    def arrive(dbs):
        for db in dbs:
            for dc in range(1, n_col):
                for p in range(2):
                    from_core(db, dc, p).wait_recv()

    def apply_gain(h):
        @pl.loop(0, half // 64)
        def _(r):
            rows = pl.ds(pl.multiple_of(h * half + r * 64, 64), 64)
            for q in range(depth // 128):
                cols = slice(q * 128, (q + 1) * 128)
                scaled[rows, cols] = (raw[rows, cols].astype(jnp.float32) * gain[:, cols].astype(
                    jnp.float32)).astype(jnp.bfloat16)

    def sq_copy(h, slot):
        return pltpu.make_async_remote_copy(
            sq_own.at[h], sq_recv.at[slot], sq_send.at[h], sq_rsem.at[slot],
            device_id={"aa": h * (n - 1)}, device_id_type=MESH)

    def squares(h):
        @pl.loop(0, half // 128)
        def _(r):
            rows = pl.ds(pl.multiple_of(h * half + r * 128, 128), 128)
            total = jnp.zeros((128, 128), jnp.float32)
            for q in range(depth // 128):
                value = raw[rows, q * 128:(q + 1) * 128].astype(jnp.float32)
                total = total + value * value
            line = jnp.sum(jnp.transpose(total), axis=0, keepdims=True)
            sq_own[h, r] = jnp.broadcast_to(line, (8, 128))

        @pl.when(a != h * (n - 1))
        def _():
            sq_copy(h, a).start()

    def hop(h):
        return jnp.where(h == 0, n - 1 - a, a)

    sub = half // n_col

    def part_copy(h, k, cc):
        to = jnp.where(h == 0, jnp.maximum(a - 1, 0), jnp.minimum(a + 1, n - 1))
        rows = pl.ds(cc * sub, sub)
        return pltpu.make_async_remote_copy(
            send.at[h, k, rows], recv.at[h, k, rows], part_send.at[h, k, cc],
            part_recv.at[h, k, cc], device_id={"aa": to}, device_id_type=MESH)

    def multiply(h, j):
        left = scaled[pl.ds(pl.multiple_of(h * half, half), half), :]
        acc[h, j, :, :tu] = jnp.dot(left, gate_v[j], preferred_element_type=jnp.float32)
        acc[h, j, :, tu:] = jnp.dot(left, up_v[j], preferred_element_type=jnp.float32)

        @pl.when(hop(h) == 0)
        def _():
            for cc in range(n_col):
                rows = slice(cc * sub, (cc + 1) * sub)
                send[h, j, rows, :] = acc[h, j, rows, :].astype(jnp.bfloat16)
                part_copy(h, j, cc).start()

    def hid_copy(h, dd, cc, i):
        index = cc * dests + dd
        first, count = (0, late) if i == 0 else (late + i - 1, 1)
        from_cols = pl.ds(first * tu, count * tu)
        to_cols = pl.ds(pl.multiple_of(c * width + first * tu, tu), count * tu)
        return pltpu.make_async_remote_copy(
            hid.at[pl.ds(index * out_rows, out_rows), from_cols], out.at[:, to_cols],
            hid_send.at[index, i], out_recv.at[c, i],
            device_id={"aa": h * dests + dd, "col": cc}, device_id_type=MESH)

    def elsewhere(h, dd, cc):
        return (a != h * dests + dd) | (c != cc)

    def send_hidden(h, i):
        for dd in range(dests):
            for cc in range(n_col):
                @pl.when(elsewhere(h, dd, cc))
                def _():
                    hid_copy(h, dd, cc, i).start()

    def find_factor(h):
        total = sq_own[h]
        for off in range(1, n):
            d = lax.rem(a + off, n)
            sq_copy(h, d).wait_recv()
            total = total + sq_recv[d]
        rate = lax.rsqrt(total / (depth * n) + EPSILON)
        for r in range(half // 128):
            factor[r * 128:(r + 1) * 128, :] = jnp.transpose(
                jnp.broadcast_to(rate[r, 0:1, :], (128, 128)))

    def finish(h, k, cc):
        rows = slice(cc * sub, (cc + 1) * sub)
        scale = factor[rows, :]
        for q in range(tu // 128):
            at = slice(q * 128, (q + 1) * 128)
            up_at = slice(tu + q * 128, tu + (q + 1) * 128)
            gate = (acc[h, k, rows, at] + recv[h, k, rows, at].astype(jnp.float32)) * scale
            up = (acc[h, k, rows, up_at] + recv[h, k, rows, up_at].astype(jnp.float32)) * scale
            cols = pl.ds(pl.multiple_of(k * tu + q * 128, 128), 128)
            hid[rows, cols] = (gate / (1.0 + jnp.exp(-gate)) * up).astype(jnp.bfloat16)

    def handle(h, k):
        here = hop(h)

        @pl.when((here > 0) & (here < n - 1))
        def _():
            for cc in range(n_col):
                part_copy(h, k, cc).wait_recv()
                rows = slice(cc * sub, (cc + 1) * sub)
                send[h, k, rows, :] = (
                    acc[h, k, rows, :] + recv[h, k, rows, :].astype(jnp.float32)
                ).astype(jnp.bfloat16)
                part_copy(h, k, cc).start()

        @pl.when(here == n - 1)
        def _():
            @pl.when(k == 0)
            def _():
                find_factor(h)

            for cc in range(n_col):
                part_copy(h, k, cc).wait_recv()
                finish(h, k, cc)

            @pl.when(k == late - 1)
            def _():
                @pl.loop(0, tiles)
                def _(j):
                    for cc in range(n_col):
                        part_copy(1 - h, j, cc).wait_send()

                send_hidden(h, 0)

            for i in range(1, tiles - late + 1):
                @pl.when(k == late + i - 1)
                def _():
                    send_hidden(h, i)

    near = b // (n_ba // 2)
    far = 1 - near

    for p in range(2):
        for db in range(1, n_ba):
            to_chip(db, p).start()
        for dc in range(1, n_col):
            to_core(0, dc, p).start()
    own.wait()
    if n_ba > 2:
        for p in range(2):
            forward(p)
        arrive(range(n_ba))
    else:
        arrive([0])
    apply_gain(near)

    @pl.loop(0, ahead)
    def _(j):
        for copy in weight_copies(j):
            copy.wait()
        multiply(near, j)
        if n_ba == 2:
            for p in range(2):
                @pl.when(j == (p + 1) * ahead // 2 - 1)
                def _():
                    forward(p)

    squares(near)
    if n_ba == 2:
        arrive([1])
    apply_gain(far)

    @pl.loop(0, tiles + (n - 1) * LAG)
    def _(s):
        @pl.when(s < tiles)
        def _():
            multiply(far, s)

        @pl.when(s == 0)
        def _():
            squares(far)

        @pl.when(s + ahead < tiles)
        def _():
            for copy in weight_copies(s + ahead):
                copy.wait()
            multiply(near, s + ahead)

        for h, k in ((near, s - (hop(near) - 1) * LAG), (far, s - hop(far) * LAG)):
            @pl.when((k >= 0) & (k < tiles) & (hop(h) > 0))
            def _():
                handle(h, k)

    finisher = (a == 0) | (a == n - 1)

    @pl.when(finisher)
    def _():
        ours = c * dests + jnp.where(a == 0, 0, dests - 1)
        out[:, pl.ds(pl.multiple_of(c * width, tu), width)] = hid[
            pl.ds(pl.multiple_of(ours * out_rows, out_rows), out_rows), :]
        side = jnp.where(a == 0, 0, 1)
        for dd in range(dests):
            for cc in range(n_col):
                @pl.when(elsewhere(side, dd, cc))
                def _():
                    for i in range(tiles - late + 1):
                        hid_copy(side, dd, cc, i).wait_send()

    @pl.when(jnp.logical_not(finisher))
    def _():
        @pl.loop(0, tiles)
        def _(k):
            for h in range(2):
                for cc in range(n_col):
                    part_copy(h, k, cc).wait_send()

    for p in range(2):
        for db in range(1, n_ba):
            to_chip(db, p).wait_send()
        for db in range(n_ba):
            for dc in range(1, n_col):
                to_core(db, dc, p).wait_send()
    for h in range(2):
        @pl.when(a != h * (n - 1))
        def _():
            sq_copy(h, a).wait_send()

    for cc in range(n_col):
        @pl.when(jnp.logical_not(finisher & (c == cc)))
        def _():
            for i in range(tiles - late + 1):
                first, count = (0, late) if i == 0 else (late + i - 1, 1)
                pltpu.make_async_remote_copy(
                    hid.at[pl.ds(0, out_rows), pl.ds(0, count * tu)],
                    out.at[:, pl.ds(cc * width + first * tu, count * tu)],
                    hid_send.at[0, i], out_recv.at[cc, i],
                    device_id={"col": cc}, device_id_type=MESH).wait_recv()


def shards(sizes, tokens, norm_gain, gate_weight, up_weight):
    n, n_ba, n_col, tiles = sizes
    own_rows, depth = tokens.shape
    width = gate_weight.shape[1]
    tu = width // tiles
    rows = own_rows * n_ba * n_col
    half = rows // 2
    out_rows = rows // (n * n_col)
    bf16, f32 = jnp.bfloat16, jnp.float32
    dma = pltpu.SemaphoreType.DMA
    any_space = pl.BlockSpec(memory_space=pl.ANY)
    vmem = pl.BlockSpec(memory_space=pltpu.VMEM)
    flops = 2 * rows * depth * 2 * width
    return pl.pallas_call(
        functools.partial(kernel, sizes),
        out_shape=jax.ShapeDtypeStruct((out_rows, width * n_col), bf16),
        in_specs=[any_space, vmem, any_space, any_space],
        out_specs=vmem,
        scratch_shapes=[
            pltpu.VMEM((rows, depth), bf16),
            pltpu.VMEM((rows, depth), bf16),
            pltpu.VMEM((tiles, depth, tu), bf16),
            pltpu.VMEM((tiles, depth, tu), bf16),
            pltpu.VMEM((2, tiles, half, 2 * tu), f32),
            pltpu.VMEM((2, tiles, half, 2 * tu), bf16),
            pltpu.VMEM((2, tiles, half, 2 * tu), bf16),
            pltpu.VMEM((half, width), bf16),
            pltpu.VMEM((2, half // 128, 8, 128), f32),
            pltpu.VMEM((n, half // 128, 8, 128), f32),
            pltpu.VMEM((half, 128), f32),
            dma((2, tiles)),
            dma,
            dma((n_ba, 2)),
            dma((n_ba, 2)),
            dma((n_ba, n_col, 2)),
            dma((n_ba, n_col, 2)),
            dma((2, tiles, n_col)),
            dma((2, tiles, n_col)),
            dma((2,)),
            dma((n,)),
            dma((n // 2 * n_col, 4)),
            dma((n_col, 4)),
        ],
        compiler_params=pltpu.CompilerParams(
            collective_id=0, has_side_effects=True, vmem_limit_bytes=60 * 1024 * 1024),
        cost_estimate=pl.CostEstimate(
            flops=flops, bytes_accessed=4 * depth * width, transcendentals=half * width),
    )(tokens, norm_gain.reshape(1, depth), gate_weight, up_weight)


def solution(mesh):
    def run(tokens, norm_gain, gate_weight, up_weight):
        n, n_ba, n_col = mesh.shape["aa"], mesh.shape["ba"], mesh.shape["col"]
        width = gate_weight.shape[1] // (n_ba * n_col)
        tu = 256 if width % 256 == 0 and width > 1024 else 128
        sizes = (n, n_ba, n_col, width // tu)
        return jax.shard_map(
            functools.partial(shards, sizes),
            mesh=mesh,
            in_specs=(
                P(("groups", "col", "ba"), "aa"),
                P("aa"),
                P("aa", ("ba", "col")),
                P("aa", ("ba", "col")),
            ),
            out_specs=P(("groups", "col", "aa"), "ba"),
            check_vma=False,
        )(tokens, norm_gain, gate_weight, up_weight)

    return run
```

```python
import functools

import jax
import jax.numpy as jnp
from jax import lax
from jax.experimental import pallas as pl
from jax.experimental.pallas import tpu as pltpu
from jax.sharding import PartitionSpec as P

MESH = pl.DeviceIdType.MESH
EPSILON = 1e-05
AHEAD = 6


def kernel(sizes, tokens, gain, gate_w, up_w, out, raw, scaled, gate_v, up_v, acc, recv, send,
           hid, sq_own, sq_recv, factor, w_sem, own_sem, x_send, x_recv, c_send, c_recv,
           part_send, part_recv, sq_send, sq_rsem, hid_send, out_recv):
    n, n_ba, n_col, tiles = sizes
    a, b, c = lax.axis_index("aa"), lax.axis_index("ba"), lax.axis_index("col")
    own_rows, depth = tokens.shape
    width = gate_w.shape[1]
    tu = width // tiles
    half = scaled.shape[0] // 2
    out_rows = out.shape[0]
    dests = n // 2
    ahead = min(AHEAD, tiles)
    late = tiles - 3 if n > 2 else tiles

    def start_of(bb, cc):
        per_half = n_ba // 2
        row = (bb // per_half) * half + cc * (half // n_col) + (bb % per_half) * own_rows
        return pl.multiple_of(row, own_rows)

    def block(bb, cc):
        return raw.at[pl.ds(start_of(bb, cc), own_rows)]

    def weight_copies(j):
        cols = pl.ds(pl.multiple_of(j * tu, tu), tu)
        return (pltpu.make_async_copy(gate_w.at[:, cols], gate_v.at[j], w_sem.at[0, j]),
                pltpu.make_async_copy(up_w.at[:, cols], up_v.at[j], w_sem.at[1, j]))

    barrier = pltpu.get_barrier_semaphore()
    peers = 0
    for da in range(n):
        for dc in range(n_col):
            if da or dc:
                pl.semaphore_signal(
                    barrier, inc=1, device_id_type=MESH,
                    device_id={"aa": lax.rem(a + da, n), "col": lax.rem(c + dc, n_col)})
                peers += 1
    for db in range(1, n_ba):
        pl.semaphore_signal(barrier, inc=1, device_id={"ba": lax.rem(b + db, n_ba)},
                            device_id_type=MESH)
        peers += 1

    own = pltpu.make_async_copy(tokens, block(b, c), own_sem)
    own.start()

    @pl.loop(0, tiles)
    def _(j):
        for copy in weight_copies(j):
            copy.start()

    pl.semaphore_wait(barrier, peers)

    def piece(ref, p):
        return ref.at[pl.ds(p * (own_rows // 2), own_rows // 2)]

    def back(i, d, count):
        return lax.rem(i - d + count, count)

    def to_chip(db, p, source=None):
        spot = block(b if source is None else source, c)
        return pltpu.make_async_remote_copy(
            piece(tokens, p), piece(spot, p), x_send.at[db, p], x_recv.at[db, p],
            device_id={"ba": lax.rem(b + db, n_ba)}, device_id_type=MESH)

    def to_core(db, dc, p):
        spot = piece(block(back(b, db, n_ba), c), p)
        return pltpu.make_async_remote_copy(
            piece(tokens, p) if db == 0 else spot, spot, c_send.at[db, dc, p],
            c_recv.at[db, dc, p],
            device_id={"col": lax.rem(c + dc, n_col)}, device_id_type=MESH)

    def from_core(db, dc, p):
        spot = piece(block(back(b, db, n_ba), back(c, dc, n_col)), p)
        return pltpu.make_async_remote_copy(
            piece(tokens, p), spot, c_send.at[db, dc, p], c_recv.at[db, dc, p],
            device_id={"col": lax.rem(c + dc, n_col)}, device_id_type=MESH)

    def forward(p):
        for db in range(1, n_ba):
            to_chip(db, p, back(b, db, n_ba)).wait_recv()
            for dc in range(1, n_col):
                to_core(db, dc, p).start()

    def arrive(dbs):
        for db in dbs:
            for dc in range(1, n_col):
                for p in range(2):
                    from_core(db, dc, p).wait_recv()

    def apply_gain(h):
        @pl.loop(0, half // 64)
        def _(r):
            rows = pl.ds(pl.multiple_of(h * half + r * 64, 64), 64)
            for q in range(depth // 128):
                cols = slice(q * 128, (q + 1) * 128)
                scaled[rows, cols] = (raw[rows, cols].astype(jnp.float32) * gain[cols].astype(
                    jnp.float32)).astype(jnp.bfloat16)

    def sq_copy(h, slot):
        return pltpu.make_async_remote_copy(
            sq_own.at[h], sq_recv.at[slot], sq_send.at[h], sq_rsem.at[slot],
            device_id={"aa": h * (n - 1)}, device_id_type=MESH)

    def squares(h):
        @pl.loop(0, half // 128)
        def _(r):
            rows = pl.ds(pl.multiple_of(h * half + r * 128, 128), 128)
            total = jnp.zeros((128, 128), jnp.float32)
            for q in range(depth // 128):
                value = raw[rows, q * 128:(q + 1) * 128].astype(jnp.float32)
                total = total + value * value
            line = jnp.sum(jnp.transpose(total), axis=0, keepdims=True)
            sq_own[h, r] = jnp.broadcast_to(line, (8, 128))

        @pl.when(a != h * (n - 1))
        def _():
            sq_copy(h, a).start()

    def hop(h):
        return jnp.where(h == 0, n - 1 - a, a)

    sub = half // n_col

    def part_copy(h, k, cc):
        to = jnp.where(h == 0, jnp.maximum(a - 1, 0), jnp.minimum(a + 1, n - 1))
        rows = pl.ds(cc * sub, sub)
        return pltpu.make_async_remote_copy(
            send.at[h, k, rows], recv.at[h, k, rows], part_send.at[h, k, cc],
            part_recv.at[h, k, cc], device_id={"aa": to}, device_id_type=MESH)

    def multiply(h, j):
        left = scaled[pl.ds(pl.multiple_of(h * half, half), half), :]
        acc[h, j, :, :tu] = jnp.dot(left, gate_v[j], preferred_element_type=jnp.float32)
        acc[h, j, :, tu:] = jnp.dot(left, up_v[j], preferred_element_type=jnp.float32)

        @pl.when(hop(h) == 0)
        def _():
            for cc in range(n_col):
                rows = slice(cc * sub, (cc + 1) * sub)
                send[h, j, rows, :] = acc[h, j, rows, :].astype(jnp.bfloat16)
                part_copy(h, j, cc).start()

    def hid_copy(h, dd, cc, i):
        index = cc * dests + dd
        first, count = (0, late) if i == 0 else (late + i - 1, 1)
        from_cols = pl.ds(first * tu, count * tu)
        to_cols = pl.ds(pl.multiple_of(c * width + first * tu, tu), count * tu)
        return pltpu.make_async_remote_copy(
            hid.at[pl.ds(index * out_rows, out_rows), from_cols], out.at[:, to_cols],
            hid_send.at[index, i], out_recv.at[c, i],
            device_id={"aa": h * dests + dd, "col": cc}, device_id_type=MESH)

    def elsewhere(h, dd, cc):
        return (a != h * dests + dd) | (c != cc)

    def send_hidden(h, i):
        for dd in range(dests):
            for cc in range(n_col):
                @pl.when(elsewhere(h, dd, cc))
                def _():
                    hid_copy(h, dd, cc, i).start()

    def find_factor(h):
        total = sq_own[h]
        for off in range(1, n):
            d = lax.rem(a + off, n)
            sq_copy(h, d).wait_recv()
            total = total + sq_recv[d]
        rate = lax.rsqrt(total / (depth * n) + EPSILON)
        for r in range(half // 128):
            factor[r * 128:(r + 1) * 128, :] = jnp.transpose(
                jnp.broadcast_to(rate[r, 0:1, :], (128, 128)))

    def finish(h, k, cc):
        rows = slice(cc * sub, (cc + 1) * sub)
        scale = factor[rows, :]
        for q in range(tu // 128):
            at = slice(q * 128, (q + 1) * 128)
            up_at = slice(tu + q * 128, tu + (q + 1) * 128)
            gate = (acc[h, k, rows, at] + recv[h, k, rows, at].astype(jnp.float32)) * scale
            up = (acc[h, k, rows, up_at] + recv[h, k, rows, up_at].astype(jnp.float32)) * scale
            cols = pl.ds(pl.multiple_of(k * tu + q * 128, 128), 128)
            hid[rows, cols] = (gate / (1.0 + jnp.exp(-gate)) * up).astype(jnp.bfloat16)

    def handle(h, k):
        here = hop(h)

        @pl.when((here > 0) & (here < n - 1))
        def _():
            for cc in range(n_col):
                part_copy(h, k, cc).wait_recv()
                rows = slice(cc * sub, (cc + 1) * sub)
                send[h, k, rows, :] = (
                    acc[h, k, rows, :] + recv[h, k, rows, :].astype(jnp.float32)
                ).astype(jnp.bfloat16)
                part_copy(h, k, cc).start()

        @pl.when(here == n - 1)
        def _():
            @pl.when(k == 0)
            def _():
                find_factor(h)

            for cc in range(n_col):
                part_copy(h, k, cc).wait_recv()
                finish(h, k, cc)

            @pl.when(k == late - 1)
            def _():
                @pl.loop(0, tiles)
                def _(j):
                    for cc in range(n_col):
                        part_copy(1 - h, j, cc).wait_send()

                send_hidden(h, 0)

            for i in range(1, tiles - late + 1):
                @pl.when(k == late + i - 1)
                def _():
                    send_hidden(h, i)

    near = b // (n_ba // 2)
    far = 1 - near
    near_lag = hop(near) - 1 + jnp.where(hop(near) == n - 1, 2, 0)
    far_lag = jnp.where(hop(far) == 0, 0, 2 * hop(far) - 1)

    for p in range(2):
        for db in range(1, n_ba):
            to_chip(db, p).start()
        for dc in range(1, n_col):
            to_core(0, dc, p).start()
    own.wait()
    if n_ba > 2:
        for p in range(2):
            forward(p)
        arrive(range(n_ba))
    else:
        arrive([0])
    apply_gain(near)

    @pl.loop(0, ahead)
    def _(j):
        for copy in weight_copies(j):
            copy.wait()
        multiply(near, j)
        if n_ba == 2:
            for p in range(2):
                @pl.when(j == (p + 1) * ahead // 2 - 1)
                def _():
                    forward(p)

    squares(near)
    if n_ba == 2:
        arrive([1])
    apply_gain(far)

    @pl.loop(0, tiles + 2 * n)
    def _(s):
        @pl.when(s < tiles)
        def _():
            multiply(far, s)

        @pl.when(s == 0)
        def _():
            squares(far)

        @pl.when(s + ahead < tiles)
        def _():
            for copy in weight_copies(s + ahead):
                copy.wait()
            multiply(near, s + ahead)

        for h, k in ((near, s - near_lag), (far, s - far_lag)):
            @pl.when((k >= 0) & (k < tiles) & (hop(h) > 0))
            def _():
                handle(h, k)

    finisher = (a == 0) | (a == n - 1)

    @pl.when(finisher)
    def _():
        ours = c * dests + jnp.where(a == 0, 0, dests - 1)
        out[:, pl.ds(pl.multiple_of(c * width, tu), width)] = hid[
            pl.ds(pl.multiple_of(ours * out_rows, out_rows), out_rows), :]
        side = jnp.where(a == 0, 0, 1)
        for dd in range(dests):
            for cc in range(n_col):
                @pl.when(elsewhere(side, dd, cc))
                def _():
                    for i in range(tiles - late + 1):
                        hid_copy(side, dd, cc, i).wait_send()

    @pl.when(jnp.logical_not(finisher))
    def _():
        @pl.loop(0, tiles)
        def _(k):
            for h in range(2):
                for cc in range(n_col):
                    part_copy(h, k, cc).wait_send()

    for p in range(2):
        for db in range(1, n_ba):
            to_chip(db, p).wait_send()
        for db in range(n_ba):
            for dc in range(1, n_col):
                to_core(db, dc, p).wait_send()
    for h in range(2):
        @pl.when(a != h * (n - 1))
        def _():
            sq_copy(h, a).wait_send()

    for cc in range(n_col):
        @pl.when(jnp.logical_not(finisher & (c == cc)))
        def _():
            for i in range(tiles - late + 1):
                first, count = (0, late) if i == 0 else (late + i - 1, 1)
                pltpu.make_async_remote_copy(
                    hid.at[pl.ds(0, out_rows), pl.ds(0, count * tu)],
                    out.at[:, pl.ds(cc * width + first * tu, count * tu)],
                    hid_send.at[0, i], out_recv.at[cc, i],
                    device_id={"col": cc}, device_id_type=MESH).wait_recv()


def shards(sizes, tokens, norm_gain, gate_weight, up_weight):
    n, n_ba, n_col, tiles = sizes
    own_rows, depth = tokens.shape
    width = gate_weight.shape[1]
    tu = width // tiles
    rows = own_rows * n_ba * n_col
    half = rows // 2
    out_rows = rows // (n * n_col)
    bf16, f32 = jnp.bfloat16, jnp.float32
    dma = pltpu.SemaphoreType.DMA
    any_space = pl.BlockSpec(memory_space=pl.ANY)
    vmem = pl.BlockSpec(memory_space=pltpu.VMEM)
    flops = 2 * rows * depth * 2 * width
    return pl.pallas_call(
        functools.partial(kernel, sizes),
        out_shape=jax.ShapeDtypeStruct((out_rows, width * n_col), bf16),
        in_specs=[any_space, vmem, any_space, any_space],
        out_specs=vmem,
        scratch_shapes=[
            pltpu.VMEM((rows, depth), bf16),
            pltpu.VMEM((rows, depth), bf16),
            pltpu.VMEM((tiles, depth, tu), bf16),
            pltpu.VMEM((tiles, depth, tu), bf16),
            pltpu.VMEM((2, tiles, half, 2 * tu), f32),
            pltpu.VMEM((2, tiles, half, 2 * tu), bf16),
            pltpu.VMEM((2, tiles, half, 2 * tu), bf16),
            pltpu.VMEM((half, width), bf16),
            pltpu.VMEM((2, half // 128, 8, 128), f32),
            pltpu.VMEM((n, half // 128, 8, 128), f32),
            pltpu.VMEM((half, 128), f32),
            dma((2, tiles)),
            dma,
            dma((n_ba, 2)),
            dma((n_ba, 2)),
            dma((n_ba, n_col, 2)),
            dma((n_ba, n_col, 2)),
            dma((2, tiles, n_col)),
            dma((2, tiles, n_col)),
            dma((2,)),
            dma((n,)),
            dma((n // 2 * n_col, 4)),
            dma((n_col, 4)),
        ],
        compiler_params=pltpu.CompilerParams(
            collective_id=0, has_side_effects=True, vmem_limit_bytes=60 * 1024 * 1024),
        cost_estimate=pl.CostEstimate(
            flops=flops, bytes_accessed=4 * depth * width, transcendentals=half * width),
    )(tokens, norm_gain, gate_weight, up_weight)


def solution(mesh):
    def run(tokens, norm_gain, gate_weight, up_weight):
        n, n_ba, n_col = mesh.shape["aa"], mesh.shape["ba"], mesh.shape["col"]
        width = gate_weight.shape[1] // (n_ba * n_col)
        tu = 256 if width % 256 == 0 and width > 1024 else 128
        sizes = (n, n_ba, n_col, width // tu)
        return jax.shard_map(
            functools.partial(shards, sizes),
            mesh=mesh,
            in_specs=(
                P(("groups", "col", "ba"), "aa"),
                P("aa"),
                P("aa", ("ba", "col")),
                P("aa", ("ba", "col")),
            ),
            out_specs=P(("groups", "col", "aa"), "ba"),
            check_vma=False,
        )(tokens, norm_gain, gate_weight, up_weight)

    return run
```

```python
import functools

import jax
import jax.numpy as jnp
from jax import lax
from jax.experimental import pallas as pl
from jax.experimental.pallas import tpu as pltpu
from jax.sharding import PartitionSpec as P

MESH = pl.DeviceIdType.MESH
EPSILON = 1e-05
AHEAD = 6


def kernel(sizes, tokens, gain, gate_w, up_w, out, raw, scaled, gate_v, up_v, acc, recv, send,
           hid, sq_own, sq_recv, factor, w_sem, own_sem, x_send, x_recv, c_send, c_recv,
           part_send, part_recv, sq_send, sq_rsem, hid_send, out_recv):
    n, n_ba, n_col, tiles = sizes
    a, b, c = lax.axis_index("aa"), lax.axis_index("ba"), lax.axis_index("col")
    own_rows, depth = tokens.shape
    width = gate_w.shape[1]
    tu = width // tiles
    half = scaled.shape[0] // 2
    out_rows = out.shape[0]
    dests = n // 2
    ahead = min(AHEAD, tiles)
    late = tiles - 3 if n > 2 else tiles

    def start_of(bb, cc):
        per_half = n_ba // 2
        row = (bb // per_half) * half + cc * (half // n_col) + (bb % per_half) * own_rows
        return pl.multiple_of(row, own_rows)

    def block(bb, cc):
        return raw.at[pl.ds(start_of(bb, cc), own_rows)]

    def weight_copies(j):
        cols = pl.ds(pl.multiple_of(j * tu, tu), tu)
        return (pltpu.make_async_copy(gate_w.at[:, cols], gate_v.at[j], w_sem.at[0, j]),
                pltpu.make_async_copy(up_w.at[:, cols], up_v.at[j], w_sem.at[1, j]))

    barrier = pltpu.get_barrier_semaphore()
    peers = 0
    for da in range(n):
        for dc in range(n_col):
            if da or dc:
                pl.semaphore_signal(
                    barrier, inc=1, device_id_type=MESH,
                    device_id={"aa": lax.rem(a + da, n), "col": lax.rem(c + dc, n_col)})
                peers += 1
    for db in range(1, n_ba):
        pl.semaphore_signal(barrier, inc=1, device_id={"ba": lax.rem(b + db, n_ba)},
                            device_id_type=MESH)
        peers += 1

    own = pltpu.make_async_copy(tokens, block(b, c), own_sem)
    own.start()

    @pl.loop(0, tiles)
    def _(j):
        for copy in weight_copies(j):
            copy.start()

    pl.semaphore_wait(barrier, peers)

    def piece(ref, p):
        return ref.at[pl.ds(p * (own_rows // 2), own_rows // 2)]

    def back(i, d, count):
        return lax.rem(i - d + count, count)

    def to_chip(db, p, source=None):
        spot = block(b if source is None else source, c)
        return pltpu.make_async_remote_copy(
            piece(tokens, p), piece(spot, p), x_send.at[db, p], x_recv.at[db, p],
            device_id={"ba": lax.rem(b + db, n_ba)}, device_id_type=MESH)

    def to_core(db, dc, p):
        spot = piece(block(back(b, db, n_ba), c), p)
        return pltpu.make_async_remote_copy(
            piece(tokens, p) if db == 0 else spot, spot, c_send.at[db, dc, p],
            c_recv.at[db, dc, p],
            device_id={"col": lax.rem(c + dc, n_col)}, device_id_type=MESH)

    def from_core(db, dc, p):
        spot = piece(block(back(b, db, n_ba), back(c, dc, n_col)), p)
        return pltpu.make_async_remote_copy(
            piece(tokens, p), spot, c_send.at[db, dc, p], c_recv.at[db, dc, p],
            device_id={"col": lax.rem(c + dc, n_col)}, device_id_type=MESH)

    def forward(p):
        for db in range(1, n_ba):
            to_chip(db, p, back(b, db, n_ba)).wait_recv()
            for dc in range(1, n_col):
                to_core(db, dc, p).start()

    def arrive(dbs):
        for db in dbs:
            for dc in range(1, n_col):
                for p in range(2):
                    from_core(db, dc, p).wait_recv()

    def apply_gain(h):
        @pl.loop(0, half // 64)
        def _(r):
            rows = pl.ds(pl.multiple_of(h * half + r * 64, 64), 64)
            for q in range(depth // 128):
                cols = slice(q * 128, (q + 1) * 128)
                scaled[rows, cols] = (raw[rows, cols].astype(jnp.float32) * gain[cols].astype(
                    jnp.float32)).astype(jnp.bfloat16)

    def sq_copy(h, slot):
        return pltpu.make_async_remote_copy(
            sq_own.at[h], sq_recv.at[slot], sq_send.at[h], sq_rsem.at[slot],
            device_id={"aa": h * (n - 1)}, device_id_type=MESH)

    def squares(h):
        @pl.loop(0, half // 128)
        def _(r):
            rows = pl.ds(pl.multiple_of(h * half + r * 128, 128), 128)
            total = jnp.zeros((128, 128), jnp.float32)
            for q in range(depth // 128):
                value = raw[rows, q * 128:(q + 1) * 128].astype(jnp.float32)
                total = total + value * value
            line = jnp.sum(jnp.transpose(total), axis=0, keepdims=True)
            sq_own[h, r] = jnp.broadcast_to(line, (8, 128))

        @pl.when(a != h * (n - 1))
        def _():
            sq_copy(h, a).start()

    def hop(h):
        return jnp.where(h == 0, n - 1 - a, a)

    sub = half // n_col

    def part_copy(h, k, cc):
        to = jnp.where(h == 0, jnp.maximum(a - 1, 0), jnp.minimum(a + 1, n - 1))
        rows = pl.ds(cc * sub, sub)
        return pltpu.make_async_remote_copy(
            send.at[h, k, rows], recv.at[h, k, rows], part_send.at[h, k, cc],
            part_recv.at[h, k, cc], device_id={"aa": to}, device_id_type=MESH)

    def multiply(h, j):
        left = scaled[pl.ds(pl.multiple_of(h * half, half), half), :]
        acc[h, j, :, :tu] = jnp.dot(left, gate_v[j], preferred_element_type=jnp.float32)
        acc[h, j, :, tu:] = jnp.dot(left, up_v[j], preferred_element_type=jnp.float32)

        @pl.when(hop(h) == 0)
        def _():
            for cc in range(n_col):
                rows = slice(cc * sub, (cc + 1) * sub)
                send[h, j, rows, :] = acc[h, j, rows, :].astype(jnp.bfloat16)
                part_copy(h, j, cc).start()

    def hid_copy(h, dd, cc, i):
        index = cc * dests + dd
        first, count = (0, late) if i == 0 else (late + i - 1, 1)
        from_cols = pl.ds(first * tu, count * tu)
        to_cols = pl.ds(pl.multiple_of(c * width + first * tu, tu), count * tu)
        return pltpu.make_async_remote_copy(
            hid.at[pl.ds(index * out_rows, out_rows), from_cols], out.at[:, to_cols],
            hid_send.at[index, i], out_recv.at[c, i],
            device_id={"aa": h * dests + dd, "col": cc}, device_id_type=MESH)

    def elsewhere(h, dd, cc):
        return (a != h * dests + dd) | (c != cc)

    def send_hidden(h, i):
        for dd in range(dests):
            for cc in range(n_col):
                @pl.when(elsewhere(h, dd, cc))
                def _():
                    hid_copy(h, dd, cc, i).start()

    def find_factor(h):
        total = sq_own[h]
        for off in range(1, n):
            d = lax.rem(a + off, n)
            sq_copy(h, d).wait_recv()
            total = total + sq_recv[d]
        rate = lax.rsqrt(total / (depth * n) + EPSILON)
        for r in range(half // 128):
            factor[r * 128:(r + 1) * 128, :] = jnp.transpose(
                jnp.broadcast_to(rate[r, 0:1, :], (128, 128)))

    def finish(h, k, cc):
        rows = slice(cc * sub, (cc + 1) * sub)
        scale = factor[rows, :]
        for q in range(tu // 128):
            at = slice(q * 128, (q + 1) * 128)
            up_at = slice(tu + q * 128, tu + (q + 1) * 128)
            gate = (acc[h, k, rows, at] + recv[h, k, rows, at].astype(jnp.float32)) * scale
            up = (acc[h, k, rows, up_at] + recv[h, k, rows, up_at].astype(jnp.float32)) * scale
            cols = pl.ds(pl.multiple_of(k * tu + q * 128, 128), 128)
            hid[rows, cols] = (gate / (1.0 + jnp.exp(-gate)) * up).astype(jnp.bfloat16)

    def handle(h, k):
        here = hop(h)

        @pl.when((here > 0) & (here < n - 1))
        def _():
            for cc in range(n_col):
                part_copy(h, k, cc).wait_recv()
                rows = slice(cc * sub, (cc + 1) * sub)
                send[h, k, rows, :] = (
                    acc[h, k, rows, :] + recv[h, k, rows, :].astype(jnp.float32)
                ).astype(jnp.bfloat16)
                part_copy(h, k, cc).start()

        @pl.when(here == n - 1)
        def _():
            @pl.when(k == 0)
            def _():
                find_factor(h)

            for cc in range(n_col):
                part_copy(h, k, cc).wait_recv()
                finish(h, k, cc)

            @pl.when(k == late - 1)
            def _():
                @pl.loop(0, tiles)
                def _(j):
                    for cc in range(n_col):
                        part_copy(1 - h, j, cc).wait_send()

                send_hidden(h, 0)

            for i in range(1, tiles - late + 1):
                @pl.when(k == late + i - 1)
                def _():
                    send_hidden(h, i)

    near = b // (n_ba // 2)
    far = 1 - near
    near_lag = hop(near) - 1 + jnp.where(hop(near) == n - 1, 2, 0)
    far_lag = jnp.where(hop(far) == 0, 0, 2 * hop(far) - 1)

    for p in range(2):
        for db in range(1, n_ba):
            to_chip(db, p).start()
        for dc in range(1, n_col):
            to_core(0, dc, p).start()
    own.wait()
    if n_ba > 2:
        for p in range(2):
            forward(p)
        arrive(range(n_ba))
    else:
        arrive([0])
    apply_gain(near)

    @pl.loop(0, ahead)
    def _(j):
        for copy in weight_copies(j):
            copy.wait()
        multiply(near, j)
        if n_ba == 2:
            for p in range(2):
                @pl.when(j == (p + 1) * ahead // 2 - 1)
                def _():
                    forward(p)

    if n_ba == 2:
        arrive([1])
    apply_gain(far)

    @pl.loop(0, tiles + 2 * n)
    def _(s):
        @pl.when(s < tiles)
        def _():
            multiply(far, s)

        @pl.when(s == 1)
        def _():
            squares(near)
            squares(far)

        @pl.when(s + ahead < tiles)
        def _():
            for copy in weight_copies(s + ahead):
                copy.wait()
            multiply(near, s + ahead)

        for h, k in ((near, s - near_lag), (far, s - far_lag)):
            @pl.when((k >= 0) & (k < tiles) & (hop(h) > 0))
            def _():
                handle(h, k)

    finisher = (a == 0) | (a == n - 1)

    @pl.when(finisher)
    def _():
        ours = c * dests + jnp.where(a == 0, 0, dests - 1)
        out[:, pl.ds(pl.multiple_of(c * width, tu), width)] = hid[
            pl.ds(pl.multiple_of(ours * out_rows, out_rows), out_rows), :]
        side = jnp.where(a == 0, 0, 1)
        for dd in range(dests):
            for cc in range(n_col):
                @pl.when(elsewhere(side, dd, cc))
                def _():
                    for i in range(tiles - late + 1):
                        hid_copy(side, dd, cc, i).wait_send()

    @pl.when(jnp.logical_not(finisher))
    def _():
        @pl.loop(0, tiles)
        def _(k):
            for h in range(2):
                for cc in range(n_col):
                    part_copy(h, k, cc).wait_send()

    for p in range(2):
        for db in range(1, n_ba):
            to_chip(db, p).wait_send()
        for db in range(n_ba):
            for dc in range(1, n_col):
                to_core(db, dc, p).wait_send()
    for h in range(2):
        @pl.when(a != h * (n - 1))
        def _():
            sq_copy(h, a).wait_send()

    for cc in range(n_col):
        @pl.when(jnp.logical_not(finisher & (c == cc)))
        def _():
            for i in range(tiles - late + 1):
                first, count = (0, late) if i == 0 else (late + i - 1, 1)
                pltpu.make_async_remote_copy(
                    hid.at[pl.ds(0, out_rows), pl.ds(0, count * tu)],
                    out.at[:, pl.ds(cc * width + first * tu, count * tu)],
                    hid_send.at[0, i], out_recv.at[cc, i],
                    device_id={"col": cc}, device_id_type=MESH).wait_recv()


def shards(sizes, tokens, norm_gain, gate_weight, up_weight):
    n, n_ba, n_col, tiles = sizes
    own_rows, depth = tokens.shape
    width = gate_weight.shape[1]
    tu = width // tiles
    rows = own_rows * n_ba * n_col
    half = rows // 2
    out_rows = rows // (n * n_col)
    bf16, f32 = jnp.bfloat16, jnp.float32
    dma = pltpu.SemaphoreType.DMA
    any_space = pl.BlockSpec(memory_space=pl.ANY)
    vmem = pl.BlockSpec(memory_space=pltpu.VMEM)
    flops = 2 * rows * depth * 2 * width
    return pl.pallas_call(
        functools.partial(kernel, sizes),
        out_shape=jax.ShapeDtypeStruct((out_rows, width * n_col), bf16),
        in_specs=[any_space, vmem, any_space, any_space],
        out_specs=vmem,
        scratch_shapes=[
            pltpu.VMEM((rows, depth), bf16),
            pltpu.VMEM((rows, depth), bf16),
            pltpu.VMEM((tiles, depth, tu), bf16),
            pltpu.VMEM((tiles, depth, tu), bf16),
            pltpu.VMEM((2, tiles, half, 2 * tu), f32),
            pltpu.VMEM((2, tiles, half, 2 * tu), bf16),
            pltpu.VMEM((2, tiles, half, 2 * tu), bf16),
            pltpu.VMEM((half, width), bf16),
            pltpu.VMEM((2, half // 128, 8, 128), f32),
            pltpu.VMEM((n, half // 128, 8, 128), f32),
            pltpu.VMEM((half, 128), f32),
            dma((2, tiles)),
            dma,
            dma((n_ba, 2)),
            dma((n_ba, 2)),
            dma((n_ba, n_col, 2)),
            dma((n_ba, n_col, 2)),
            dma((2, tiles, n_col)),
            dma((2, tiles, n_col)),
            dma((2,)),
            dma((n,)),
            dma((n // 2 * n_col, 4)),
            dma((n_col, 4)),
        ],
        compiler_params=pltpu.CompilerParams(
            collective_id=0, has_side_effects=True, vmem_limit_bytes=60 * 1024 * 1024),
        cost_estimate=pl.CostEstimate(
            flops=flops, bytes_accessed=4 * depth * width, transcendentals=half * width),
    )(tokens, norm_gain, gate_weight, up_weight)


def solution(mesh):
    def run(tokens, norm_gain, gate_weight, up_weight):
        n, n_ba, n_col = mesh.shape["aa"], mesh.shape["ba"], mesh.shape["col"]
        width = gate_weight.shape[1] // (n_ba * n_col)
        tu = 256 if width % 256 == 0 and width > 1024 else 128
        sizes = (n, n_ba, n_col, width // tu)
        return jax.shard_map(
            functools.partial(shards, sizes),
            mesh=mesh,
            in_specs=(
                P(("groups", "col", "ba"), "aa"),
                P("aa"),
                P("aa", ("ba", "col")),
                P("aa", ("ba", "col")),
            ),
            out_specs=P(("groups", "col", "aa"), "ba"),
            check_vma=False,
        )(tokens, norm_gain, gate_weight, up_weight)

    return run
```
